128 devices in a mesh: gx: 8 (over x, core), gy: 16 (over y, z).
Axes of the slice: x: 4, y: 4, z: 4, core: 2. Of those that a mesh axis runs over, the one named last changes fastest.
Arguments:
- tokens: bfloat16 [1024, 18432], P(None, ('gx', 'gy')), may hold values from -6 to 6
- w_query: bfloat16 [18432, 12288], P('gx', 'gy'), may hold values from -0.046875 to 0.046875
- w_keyvalue: bfloat16 [18432, 512], P('gx'), may hold values from -0.21875 to 0.21875
- w_output: bfloat16 [12288, 18432], P('gy', 'gx'), may hold values from -0.0546875 to 0.0546875
- key_cache: bfloat16 [1024, 1024, 256], P(('gx', 'gy')), may hold values from -400 to 400
- value_cache: bfloat16 [1024, 1024, 256], P(('gx', 'gy')), may hold values from -6 to 6
Outputs:
- layer_out: bfloat16 [1024, 18432], P(None, ('gx', 'gy'))
- new_keyvalue: bfloat16 [1024, 512], P(('gx', 'gy'))
The draws below stay inside these ranges and needn't reach their ends.
All inputs are finite; a program needn't handle non-finite values.
Results may differ from the reference program's by a relative error of at most 0.02.
Values may be sent and summed in bfloat16 or wider, within the bound.
No kernel may reach another device: no remote copies, remote signals or barrier semaphores. Data moves between devices by JAX's collectives and lax.ppermute only.
A program may use at most 128 MiB of HBM per device.

```python
import jax
import jax.numpy as jnp
from jax import lax

D = 18432
HEADS = 48
HD = 256
LEN = 1024
B = 1024
QW = 12288


def draw_key_cache(key, part):
    key = jax.random.fold_in(key, 11)
    first = jax.random.fold_in(key, 0)
    base = jnp.clip(jax.random.normal(first, (B, LEN, HD), jnp.float32), -6.0, 6.0)
    return (0.3 * base).astype(jnp.bfloat16)


def levels(own_key, shape, pieces, least, high):
    level, own = 1.0, jax.random.fold_in(own_key, 6)
    for dim, blocks in pieces:
        steps = jnp.exp(jax.random.uniform(jax.random.fold_in(own, dim), (blocks,), jnp.float32, least / len(pieces), high / len(pieces)))
        level = level * jnp.repeat(steps, shape[dim] // blocks).reshape([-1 if axis == dim else 1 for axis in range(len(shape))])
    return level


def bell_draw(stream_key, extent, scale, most, shards=(), held_as=jnp.bfloat16):
    array = scale * jax.random.normal(stream_key, extent, jnp.float32)
    if shards:
        array = array * levels(stream_key, extent, shards, -0.22, 0.18)
    return jnp.clip(array, -most, most).astype(held_as)


def setup_inputs(seed: int = 0) -> dict:
    seeds = jax.random.split(jax.random.key(seed), 7)
    tokens = bell_draw(seeds[0], (B, D), 1.0, 6.0, ((1, 128),))
    w_query = bell_draw(seeds[1], (D, QW), D ** -0.5, 0.046875, ((0, 8), (1, 16)))
    w_keyvalue = bell_draw(seeds[2], (D, 2 * HD), (D // 25) ** -0.5, 0.21875, ((0, 8),))
    w_output = bell_draw(seeds[3], (QW, D), QW ** -0.5, 0.0546875, ((0, 16), (1, 8)))
    key_cache = draw_key_cache(jax.random.fold_in(seeds[6], 71), 0)
    value_cache = bell_draw(seeds[5], (B, LEN, HD), 1.0, 6.0, ((0, 128),))
    return {"tokens": tokens, "w_query": w_query, "w_keyvalue": w_keyvalue, "w_output": w_output, "key_cache": key_cache, "value_cache": value_cache}


def attend_row(packed):
    queries, keys, values, keyvalue = packed
    score_scale = 1.0 / (HD ** 0.5)
    new_key = keyvalue[:HD]
    new_value = keyvalue[HD:]
    scores = jnp.dot(queries, keys.T, preferred_element_type=jnp.float32) * score_scale
    score_new = jnp.dot(queries, new_key, preferred_element_type=jnp.float32) * score_scale
    highest = jnp.maximum(jnp.max(scores, axis=1), score_new)
    raised = jnp.exp(scores - highest[:, None])
    raised_new = jnp.exp(score_new - highest)
    denominator = jnp.sum(raised, axis=1) + raised_new
    probs = (raised / denominator[:, None]).astype(jnp.bfloat16)
    prob_new = (raised_new / denominator).astype(jnp.bfloat16)
    mixed = jnp.dot(probs, values, preferred_element_type=jnp.float32)
    mixed = mixed + prob_new.astype(jnp.float32)[:, None] * new_value.astype(jnp.float32)[None, :]
    return mixed.astype(jnp.bfloat16)


def reference(tokens, w_query, w_keyvalue, w_output, key_cache, value_cache):
    queries = jnp.dot(tokens, w_query, preferred_element_type=jnp.float32).astype(jnp.bfloat16)
    new_keyvalue = jnp.dot(tokens, w_keyvalue, preferred_element_type=jnp.float32).astype(jnp.bfloat16)
    queries = queries.reshape(B, HEADS, HD)
    attended = lax.map(attend_row, (queries, key_cache, value_cache, new_keyvalue))
    attended = attended.reshape(B, QW)
    layer_out = jnp.dot(attended, w_output, preferred_element_type=jnp.float32).astype(jnp.bfloat16)
    return layer_out, new_keyvalue
```

```python
import jax
import jax.numpy as jnp
from jax import lax
from jax.sharding import Mesh
from jax.sharding import PartitionSpec as P

AXES = ("x", "c", "y", "z")
F32 = jnp.float32
BF16 = jnp.bfloat16


def linear(x, c, y, z):
    return ((x * 2 + c) * 4 + y) * 4 + z


def partner_pairs(axis, step):
    pairs = []
    for x in range(4):
        for c in range(2):
            for y in range(4):
                for z in range(4):
                    other = {"x": x, "y": y, "z": z}
                    other[axis] ^= (1, 3)[step ^ c]
                    pairs.append((linear(x, c, y, z), linear(other["x"], c, other["y"], other["z"])))
    return pairs


def exchange(v, axis, step):
    return lax.ppermute(v, AXES, partner_pairs(axis, step))


def core_swap(v):
    return lax.ppermute(v, "c", [(0, 1), (1, 0)])


def relative_blocks(first, second):
    c = lax.axis_index("c")
    m0 = jnp.where(c == 0, 1, 3)
    m1 = jnp.where(c == 0, 3, 1)
    blocks = []
    for p in range(16):
        at = {"y": lax.axis_index("y"), "z": lax.axis_index("z")}
        b = [(p >> i) & 1 for i in range(4)]
        at[first] = at[first] ^ (m0 * b[0]) ^ (m1 * b[1])
        at[second] = at[second] ^ (m0 * b[2]) ^ (m1 * b[3])
        blocks.append(at["y"] * 4 + at["z"])
    return blocks


def take_rows(w, blocks, n):
    return jnp.concatenate([lax.dynamic_slice_in_dim(w, b * n, n, 0) for b in blocks], axis=0)


def shards(tokens, w_query, w_keyvalue, w_output, key_cache, value_cache):
    c = lax.axis_index("c")
    column = lax.axis_index("y") * 4 + lax.axis_index("z")
    rows_dev, _, head_size = key_cache.shape
    feat = tokens.shape[1]
    kv_cols = w_keyvalue.shape[1] // 16
    q_cols = w_query.shape[1]

    by_core = tokens.T.reshape(feat, 4, 2, 128)
    own = lax.dynamic_index_in_dim(by_core, c, 2, keepdims=False).reshape(feat, 512)
    oth = lax.dynamic_index_in_dim(by_core, 1 - c, 2, keepdims=False).reshape(feat, 512)
    a, b = oth, own
    for axis_a, axis_b, step in (("z", "y", 0), ("z", "y", 1), ("y", "z", 0)):
        ra, rb = exchange(a, axis_a, step), exchange(b, axis_b, step)
        ra, rb = lax.optimization_barrier((ra, rb))
        a, b = jnp.concatenate([a, ra], 0), jnp.concatenate([b, rb], 0)
    la, lb = exchange(a, "y", 1), exchange(b, "z", 1)

    kv_own = lax.dynamic_slice_in_dim(w_keyvalue, column * kv_cols, kv_cols, 1)
    w_all = jnp.concatenate([w_query, kv_own], 1)
    wa = take_rows(w_all, relative_blocks("z", "y"), feat)
    wb = take_rows(w_all, relative_blocks("y", "z"), feat)
    half = 8 * feat

    def product(v, w):
        return lax.dot_general(v, w, (((0,), (0,)), ((), ())), preferred_element_type=F32)

    def widen(v):
        q, kv = v[:, :q_cols], v[:, q_cols:]
        hi = lax.reduce_precision(kv, 8, 7)
        return jnp.concatenate([q.astype(BF16), hi.astype(BF16), (kv - hi).astype(BF16)], 1)

    def narrow(v):
        v = v.astype(F32)
        return jnp.concatenate([v[..., :q_cols], v[..., q_cols : q_cols + kv_cols] + v[..., q_cols + kv_cols :]], -1)

    part_oth = product(a, wa[:half]) + product(la, wa[half:])
    got = core_swap(widen(part_oth))
    part_own = product(b, wb[:half]) + product(lb, wb[half:])
    part = widen(part_own + narrow(got))
    part = lax.all_to_all(part.reshape(64, rows_dev, -1), ("x", "y", "z"), 0, 0, tiled=True)
    whole = jnp.sum(narrow(part).reshape(4, 16, rows_dev, -1), axis=0).astype(BF16)
    queries = whole[:, :, :q_cols].transpose(1, 0, 2).reshape(rows_dev, -1, head_size)
    new_keyvalue = whole[:, :, q_cols:].transpose(1, 0, 2).reshape(rows_dev, -1)

    new_key = new_keyvalue[:, :head_size]
    new_value = new_keyvalue[:, head_size:]
    score_scale = 1.0 / head_size**0.5
    scores = jnp.einsum("bhe,bte->bht", queries, key_cache, preferred_element_type=F32) * score_scale
    score_new = jnp.einsum("bhe,be->bh", queries, new_key, preferred_element_type=F32) * score_scale
    highest = jnp.maximum(jnp.max(scores, axis=2), score_new)
    raised = jnp.exp(scores - highest[:, :, None])
    raised_new = jnp.exp(score_new - highest)
    denominator = jnp.sum(raised, axis=2) + raised_new
    probs = (raised / denominator[:, :, None]).astype(BF16)
    prob_new = (raised_new / denominator).astype(BF16)
    mixed = jnp.einsum("bht,bte->bhe", probs, value_cache, preferred_element_type=F32)
    mixed = mixed + prob_new.astype(F32)[:, :, None] * new_value.astype(F32)[:, None, :]
    attended = mixed.astype(BF16).reshape(rows_dev, 16, q_cols).transpose(1, 0, 2)

    spread = jnp.broadcast_to(attended[None], (4, 16, rows_dev, q_cols)).reshape(64, rows_dev, q_cols)
    mine = lax.all_to_all(spread, ("x", "y", "z"), 0, 0, tiled=True).reshape(512, q_cols)
    theirs = core_swap(mine)

    wo = take_rows(w_output.T, relative_blocks("z", "y"), feat)

    def outward(v):
        return lax.dot_general(wo, v, (((1,), (1,)), ((), ())), preferred_element_type=F32).astype(BF16)

    p = outward(mine).reshape(2, 2, 2, 2, feat, 512)
    q = outward(theirs).reshape(2, 2, 2, 2, feat, 512).transpose(2, 3, 0, 1, 4, 5)
    p, q = p.reshape(16 * feat, 512), q.reshape(16 * feat, 512)
    for axis_p, axis_q, step in (("y", "z", 1), ("y", "z", 0), ("z", "y", 1), ("z", "y", 0)):
        n = p.shape[0] // 2
        rp, rq = exchange(p[n:], axis_p, step), exchange(q[n:], axis_q, step)
        p = (p[:n].astype(F32) + rp.astype(F32)).astype(BF16)
        q = (q[:n].astype(F32) + rq.astype(F32)).astype(BF16)
        if step == 1 or axis_p == "y":
            p, q = lax.optimization_barrier((p, q))
    p, q = p.reshape(feat, 4, 128), q.reshape(feat, 4, 128)
    first = jnp.where(c == 0, p, q)
    second = jnp.where(c == 0, q, p)
    out = jnp.stack([first, second], axis=2).reshape(feat, 1024)
    return out.T, new_keyvalue


def solution(mesh):
    fine = Mesh(mesh.devices.reshape(4, 2, 4, 4), AXES)
    gx, gy = ("x", "c"), ("y", "z")
    every = (*gx, *gy)
    return jax.shard_map(
        shards,
        mesh=fine,
        in_specs=(P(None, every), P(gx, gy), P(gx, None), P(gy, gx), P(every, None, None), P(every, None, None)),
        out_specs=(P(None, every), P(every, None)),
        check_vma=False,
    )
```

```python
import jax
import jax.numpy as jnp
from jax import lax
from jax.experimental import pallas as pl
from jax.experimental.pallas import tpu as pltpu
from jax.sharding import Mesh
from jax.sharding import PartitionSpec as P

AXES = ("x", "c", "y", "z")
F32 = jnp.float32
BF16 = jnp.bfloat16


def linear(x, c, y, z):
    return ((x * 2 + c) * 4 + y) * 4 + z


def partner_pairs(axis, step):
    pairs = []
    for x in range(4):
        for c in range(2):
            for y in range(4):
                for z in range(4):
                    other = {"x": x, "y": y, "z": z}
                    other[axis] ^= (1, 3)[step ^ c]
                    pairs.append((linear(x, c, y, z), linear(other["x"], c, other["y"], other["z"])))
    return pairs


def exchange(v, axis, step):
    return lax.ppermute(v, AXES, partner_pairs(axis, step))


def core_swap(v):
    return lax.ppermute(v, "c", [(0, 1), (1, 0)])


def relative_blocks(first, second):
    c = lax.axis_index("c")
    m0 = jnp.where(c == 0, 1, 3)
    m1 = jnp.where(c == 0, 3, 1)
    blocks = []
    for p in range(16):
        at = {"y": lax.axis_index("y"), "z": lax.axis_index("z")}
        b = [(p >> i) & 1 for i in range(4)]
        at[first] = at[first] ^ (m0 * b[0]) ^ (m1 * b[1])
        at[second] = at[second] ^ (m0 * b[2]) ^ (m1 * b[3])
        blocks.append(at["y"] * 4 + at["z"])
    return blocks


def split_kernel(c_ref, t_ref, own_ref, oth_ref):
    c = c_ref[0]
    for x in range(4):
        to = pl.ds(x * 128, 128)
        own_ref[:, to] = t_ref[:, pl.ds(pl.multiple_of((2 * x + c) * 128, 128), 128)]
        oth_ref[:, to] = t_ref[:, pl.ds(pl.multiple_of((2 * x + 1 - c) * 128, 128), 128)]


def split_cores(c, t):
    rows = t.shape[0]
    return pl.pallas_call(
        split_kernel,
        in_specs=[pl.BlockSpec(memory_space=pltpu.SMEM), pl.BlockSpec(memory_space=pltpu.VMEM)],
        out_specs=[pl.BlockSpec(memory_space=pltpu.VMEM)] * 2,
        out_shape=[jax.ShapeDtypeStruct((rows, 512), t.dtype)] * 2,
    )(c.reshape(1), t)


def merge_kernel(c_ref, p_ref, rp_ref, q_ref, rq_ref, out_ref):
    c = c_ref[0]
    for x in range(4):
        at = pl.ds(x * 128, 128)
        p = p_ref[:, at].astype(F32) + rp_ref[:, at].astype(F32)
        q = q_ref[:, at].astype(F32) + rq_ref[:, at].astype(F32)
        out_ref[:, pl.ds(pl.multiple_of((2 * x + c) * 128, 128), 128)] = p.astype(BF16)
        out_ref[:, pl.ds(pl.multiple_of((2 * x + 1 - c) * 128, 128), 128)] = q.astype(BF16)


def merge_cores(c, *parts):
    return pl.pallas_call(
        merge_kernel,
        in_specs=[pl.BlockSpec(memory_space=pltpu.SMEM)] + [pl.BlockSpec(memory_space=pltpu.VMEM)] * 4,
        out_specs=pl.BlockSpec(memory_space=pltpu.VMEM),
        out_shape=jax.ShapeDtypeStruct((parts[0].shape[0], 1024), BF16),
    )(c.reshape(1), *parts)


def reorder(orders, sources, n):
    widths = [s.shape[1] for s in sources]
    n_src, n_out = len(sources), len(orders)
    shape = (16 * n, sum(widths))

    def kernel(order_ref, *refs):
        srcs, outs, sems = refs[:n_src], refs[n_src : n_src + n_out], refs[-1]
        copies = []
        for p in range(16):
            for o in range(n_out):
                start = pl.multiple_of(order_ref[o, p] * n, 16)
                at = 0
                for s in range(n_src):
                    copies.append(
                        pltpu.make_async_copy(
                            srcs[s].at[pl.ds(start, n), :],
                            outs[o].at[pl.ds(p * n, n), pl.ds(at, widths[s])],
                            sems.at[len(copies)],
                        )
                    )
                    at += widths[s]
        for copy in copies:
            copy.start()
        for copy in copies:
            copy.wait()

    total = 2 * n_out * shape[0] * shape[1] * 2
    return pl.pallas_call(
        kernel,
        in_specs=[pl.BlockSpec(memory_space=pltpu.SMEM)] + [pl.BlockSpec(memory_space=pl.ANY)] * n_src,
        out_specs=[pl.BlockSpec(memory_space=pl.ANY)] * n_out,
        out_shape=[jax.ShapeDtypeStruct(shape, sources[0].dtype)] * n_out,
        scratch_shapes=[pltpu.SemaphoreType.DMA((16 * n_out * n_src,))],
        cost_estimate=pl.CostEstimate(flops=0, bytes_accessed=total, transcendentals=0),
    )(jnp.stack([jnp.stack(o) for o in orders]), *sources)


def shards(tokens, w_query, w_keyvalue, w_output, key_cache, value_cache):
    c = lax.axis_index("c")
    column = lax.axis_index("y") * 4 + lax.axis_index("z")
    rows_dev, _, head_size = key_cache.shape
    feat = tokens.shape[1]
    kv_cols = w_keyvalue.shape[1] // 16
    q_cols = w_query.shape[1]

    own, oth = split_cores(c, tokens.T)
    a, b = oth, own
    for axis_a, axis_b, step in (("z", "y", 0), ("z", "y", 1)):
        ra, rb = exchange(a, axis_a, step), exchange(b, axis_b, step)
        ra, rb = lax.optimization_barrier((ra, rb))
        a, b = jnp.concatenate([a, ra], 0), jnp.concatenate([b, rb], 0)

    kv_own = lax.dynamic_slice_in_dim(w_keyvalue, column * kv_cols, kv_cols, 1)
    kv_own = jnp.pad(kv_own, ((0, 0), (0, 128 - kv_cols)))
    orders = [relative_blocks("z", "y"), relative_blocks("y", "z")]
    wa, wb = reorder(orders, [w_query, kv_own], feat)
    wp, wq = reorder(orders, [w_output.T], feat)
    a, b, wa, wb = lax.optimization_barrier((a, b, wa, wb))

    pa, pb = [a, exchange(a, "y", 0), exchange(a, "y", 1)], [b, exchange(b, "z", 0), exchange(b, "z", 1)]
    pa[1], pb[1], wp, wq = lax.optimization_barrier((pa[1], pb[1], wp, wq))
    pa.append(exchange(pa[1], "y", 1))
    pb.append(exchange(pb[1], "z", 1))
    quarter = 4 * feat

    def product(v, w, i):
        w = w[i * quarter : (i + 1) * quarter]
        return lax.dot_general(v, w, (((0,), (0,)), ((), ())), preferred_element_type=F32)

    part_oth = sum(product(pa[i], wa, i) for i in range(3))
    part_oth = (part_oth + product(pa[3], wa, 3)).astype(BF16)
    part_own = sum(product(pb[i], wb, i) for i in range(3))
    part_own = part_own + core_swap(part_oth).astype(F32)
    part = (part_own + product(pb[3], wb, 3)).astype(BF16)
    part = lax.all_to_all(part.reshape(64, rows_dev, -1), ("x", "y", "z"), 0, 0, tiled=True)
    whole = jnp.sum(part.astype(F32).reshape(4, 16, rows_dev, -1), axis=0).astype(BF16)
    queries = whole[:, :, :q_cols].transpose(1, 0, 2).reshape(rows_dev, -1, head_size)
    new_keyvalue = whole[:, :, q_cols : q_cols + kv_cols].transpose(1, 0, 2).reshape(rows_dev, -1)

    new_key = new_keyvalue[:, :head_size]
    new_value = new_keyvalue[:, head_size:]
    score_scale = 1.0 / head_size**0.5
    scores = jnp.einsum("bhe,bte->bht", queries, key_cache, preferred_element_type=F32) * score_scale
    score_new = jnp.einsum("bhe,be->bh", queries, new_key, preferred_element_type=F32) * score_scale
    highest = jnp.maximum(jnp.max(scores, axis=2), score_new)
    raised = jnp.exp(scores - highest[:, :, None])
    raised_new = jnp.exp(score_new - highest)
    denominator = jnp.sum(raised, axis=2) + raised_new
    probs = (raised / denominator[:, :, None]).astype(BF16)
    prob_new = (raised_new / denominator).astype(BF16)
    mixed = jnp.einsum("bht,bte->bhe", probs, value_cache, preferred_element_type=F32)
    mixed = mixed + prob_new.astype(F32)[:, :, None] * new_value.astype(F32)[:, None, :]
    attended = mixed.astype(BF16).reshape(rows_dev, 16, q_cols).transpose(1, 0, 2)

    spread = jnp.broadcast_to(attended[None], (4, 16, rows_dev, q_cols)).reshape(64, rows_dev, q_cols)
    mine = lax.all_to_all(spread, ("x", "y", "z"), 0, 0, tiled=True).reshape(512, q_cols)
    theirs = core_swap(mine)

    def outward(w, v, i):
        w = w[i * quarter : (i + 1) * quarter]
        return lax.dot_general(w, v, (((1,), (1,)), ((), ())), preferred_element_type=F32).astype(BF16)

    def add(*terms):
        return sum(t.astype(F32) for t in terms).astype(BF16)

    def scatter_start(w, v, axis):
        far = [exchange(outward(w, v, 3), axis, 1), exchange(outward(w, v, 2), axis, 1)]
        away = exchange(add(outward(w, v, 1), far[0]), axis, 0)
        return add(outward(w, v, 0), far[1], away)

    p, q = scatter_start(wp, mine, "y"), scatter_start(wq, theirs, "z")
    n = 2 * feat
    rp, rq = exchange(p[n:], "z", 1), exchange(q[n:], "y", 1)
    p, q = add(p[:n], rp), add(q[:n], rq)
    rp, rq = exchange(p[feat:], "z", 0), exchange(q[feat:], "y", 0)
    out = merge_cores(c, p[:feat], rp, q[:feat], rq)
    return out.T, new_keyvalue


def solution(mesh):
    fine = Mesh(mesh.devices.reshape(4, 2, 4, 4), AXES)
    gx, gy = ("x", "c"), ("y", "z")
    every = (*gx, *gy)
    return jax.shard_map(
        shards,
        mesh=fine,
        in_specs=(P(None, every), P(gx, gy), P(gx, None), P(gy, gx), P(every, None, None), P(every, None, None)),
        out_specs=(P(None, every), P(every, None)),
        check_vma=False,
    )
```

```python
import jax
import jax.numpy as jnp
from jax import lax
from jax.experimental import pallas as pl
from jax.experimental.pallas import tpu as pltpu
from jax.sharding import Mesh
from jax.sharding import PartitionSpec as P

AXES = ("x", "c", "y", "z")
F32 = jnp.float32
BF16 = jnp.bfloat16


def linear(x, c, y, z):
    return ((x * 2 + c) * 4 + y) * 4 + z


def partner_pairs(phase, mask):
    pairs = []
    for x in range(4):
        for c in range(2):
            for y in range(4):
                for z in range(4):
                    other = (y ^ mask, z) if phase != c else (y, z ^ mask)
                    pairs.append((linear(x, c, y, z), linear(x, c, *other)))
    return pairs


def exchange(v, phase, mask):
    return lax.ppermute(v, AXES, partner_pairs(phase, mask))


def core_swap(v):
    return lax.ppermute(v, "c", [(0, 1), (1, 0)])


MASKS = (1, 3, 2)
SMEM = pl.BlockSpec(memory_space=pltpu.SMEM)
VMEM = pl.BlockSpec(memory_space=pltpu.VMEM)


def block(i, n):
    return pl.ds(pl.multiple_of(i * n, 16), n)


def lanes(i):
    return pl.ds(pl.multiple_of(i * 128, 128), 128)


def split_kernel(c_ref, t_ref, out_ref):
    c = c_ref[0]
    for x in range(4):
        out_ref[:, x * 128 : (x + 1) * 128] = t_ref[:, lanes(2 * x + 1 - c)]
        out_ref[:, (x + 4) * 128 : (x + 5) * 128] = t_ref[:, lanes(2 * x + c)]


def split_cores(c, t):
    return pl.pallas_call(
        split_kernel, in_specs=[SMEM, VMEM], out_specs=VMEM, out_shape=jax.ShapeDtypeStruct(t.shape, t.dtype)
    )(c.reshape(1), t)


def merge_kernel(c_ref, *refs):
    c, terms, out_ref = c_ref[0], refs[:-1], refs[-1]
    for x in range(8):
        total = sum(t[:, x * 128 : (x + 1) * 128].astype(F32) for t in terms)
        out_ref[:, lanes(2 * (x % 4) + (c if x >= 4 else 1 - c))] = total.astype(BF16)


def merge_cores(c, *terms):
    return pl.pallas_call(
        merge_kernel,
        in_specs=[SMEM] + [VMEM] * len(terms),
        out_specs=VMEM,
        out_shape=jax.ShapeDtypeStruct(terms[0].shape, BF16),
    )(c.reshape(1), *terms)


def assemble_kernel(at_ref, *refs):
    n = refs[0].shape[0]
    for p in range(4):
        refs[4][block(at_ref[p], n), :] = refs[p][...]


def assemble(places, *pieces):
    n, m = pieces[0].shape
    return pl.pallas_call(
        assemble_kernel,
        in_specs=[SMEM] + [VMEM] * 4,
        out_specs=VMEM,
        out_shape=jax.ShapeDtypeStruct((4 * n, m), BF16),
    )(jnp.stack(places), *pieces)


def part_kernel(at_ref, *refs):
    terms, outs = refs[:8], refs[8:]
    n, m = terms[0].shape[0] // 4, terms[0].shape[1]
    for p in range(4):
        at = block(at_ref[p], n)
        for half in range(2):
            total = sum(t[at, :].astype(F32) for t in terms[4 * half : 4 * half + 4])
            outs[p][:, half * m : (half + 1) * m] = total.astype(BF16)


def add_and_part(places, *terms):
    n, m = terms[0].shape
    return pl.pallas_call(
        part_kernel,
        in_specs=[SMEM] + [VMEM] * 8,
        out_specs=[VMEM] * 4,
        out_shape=[jax.ShapeDtypeStruct((n // 4, 2 * m), BF16)] * 4,
        compiler_params=pltpu.CompilerParams(vmem_limit_bytes=32 * 1024 * 1024),
    )(jnp.stack(places), *terms)


def shards(tokens, w_query, w_keyvalue, w_output, key_cache, value_cache):
    c = lax.axis_index("c")
    column = lax.axis_index("y") * 4 + lax.axis_index("z")
    rows_dev, _, head_size = key_cache.shape
    feat = tokens.shape[1]
    kv_cols = w_keyvalue.shape[1] // 16
    q_cols = w_query.shape[1]

    y, z = lax.axis_index("y"), lax.axis_index("z")
    first, second = jnp.where(c == 0, z, y), jnp.where(c == 0, y, z)
    firsts, seconds = [first ^ m for m in (0, *MASKS)], [second ^ m for m in (0, *MASKS)]

    t = split_cores(c, tokens.T)
    t = assemble(firsts, t, *[exchange(t, 0, m) for m in MASKS])
    t1, t3 = exchange(t, 1, 1), exchange(t, 1, 3)
    half = t.shape[0] // 2
    low, high = exchange(t3[:half], 1, 1), exchange(t1[half:], 1, 3)

    def by_blocks(w):
        w = w.reshape(4, 4, feat, -1)
        return jnp.where(c == 0, w, w.swapaxes(0, 1)).reshape(16 * feat, -1)

    kv_own = lax.dynamic_slice_in_dim(w_keyvalue, column * kv_cols, kv_cols, 1)
    w_all = by_blocks(jnp.concatenate([w_query, jnp.pad(kv_own, ((0, 0), (0, 128 - kv_cols)))], 1))
    w_out = by_blocks(lax.optimization_barrier(w_output.T))

    def product(v, i, skip=0):
        w = lax.dynamic_slice_in_dim(w_all, i * 4 * feat + skip, v.shape[0], 0)
        return lax.dot_general(v, w, (((0,), (0,)), ((), ())), preferred_element_type=F32)

    part = product(t, seconds[0]) + product(t1, seconds[1]) + product(t3, seconds[2])
    part = part + product(low, seconds[3]) + product(high, seconds[3], half)
    part = core_swap(part[:512].astype(BF16)).astype(F32) + part[512:]
    part = part.astype(BF16)
    part = lax.all_to_all(part.reshape(64, rows_dev, -1), ("x", "y", "z"), 0, 0, tiled=True)
    whole = jnp.sum(part.astype(F32).reshape(4, 16, rows_dev, -1), axis=0).astype(BF16)
    queries = whole[:, :, :q_cols].transpose(1, 0, 2).reshape(rows_dev, -1, head_size)
    new_keyvalue = whole[:, :, q_cols : q_cols + kv_cols].transpose(1, 0, 2).reshape(rows_dev, -1)

    new_key = new_keyvalue[:, :head_size]
    new_value = new_keyvalue[:, head_size:]
    score_scale = 1.0 / head_size**0.5
    scores = jnp.einsum("bhe,bte->bht", queries, key_cache, preferred_element_type=F32) * score_scale
    score_new = jnp.einsum("bhe,be->bh", queries, new_key, preferred_element_type=F32) * score_scale
    highest = jnp.maximum(jnp.max(scores, axis=2), score_new)
    raised = jnp.exp(scores - highest[:, :, None])
    raised_new = jnp.exp(score_new - highest)
    denominator = jnp.sum(raised, axis=2) + raised_new
    probs = (raised / denominator[:, :, None]).astype(BF16)
    prob_new = (raised_new / denominator).astype(BF16)
    mixed = jnp.einsum("bht,bte->bhe", probs, value_cache, preferred_element_type=F32)
    mixed = mixed + prob_new.astype(F32)[:, :, None] * new_value.astype(F32)[:, None, :]
    attended = mixed.astype(BF16).reshape(rows_dev, 16, q_cols).transpose(1, 0, 2)

    spread = jnp.broadcast_to(attended[None], (4, 16, rows_dev, q_cols)).reshape(64, rows_dev, q_cols)
    mine = lax.all_to_all(spread, ("x", "y", "z"), 0, 0, tiled=True).reshape(512, q_cols)
    theirs = core_swap(mine)

    def outward(i, v):
        w = lax.dynamic_slice_in_dim(w_out, i * 4 * feat, 4 * feat, 0)
        return lax.dot_general(w, v, (((1,), (1,)), ((), ())), preferred_element_type=F32).astype(BF16)

    terms = []
    for v in (theirs, mine):
        terms.append(outward(seconds[0], v))
        terms += [exchange(outward(seconds[i + 1], v), 1, MASKS[i]) for i in range(3)]
    keep, *away = add_and_part(firsts, *terms)
    out = merge_cores(c, keep, *[exchange(v, 0, m) for v, m in zip(away, MASKS)])
    return out.T, new_keyvalue


def solution(mesh):
    fine = Mesh(mesh.devices.reshape(4, 2, 4, 4), AXES)
    gx, gy = ("x", "c"), ("y", "z")
    every = (*gx, *gy)
    return jax.shard_map(
        shards,
        mesh=fine,
        in_specs=(P(None, every), P(gx, gy), P(gx, None), P(gy, gx), P(every, None, None), P(every, None, None)),
        out_specs=(P(None, every), P(every, None)),
        check_vma=False,
    )
```

```python
import functools

import jax
import jax.numpy as jnp
from jax import lax
from jax.experimental import pallas as pl
from jax.experimental.pallas import tpu as pltpu
from jax.sharding import Mesh
from jax.sharding import PartitionSpec as P

AXES = ("x", "c", "y", "z")
F32 = jnp.float32
BF16 = jnp.bfloat16


def linear(x, c, y, z):
    return ((x * 2 + c) * 4 + y) * 4 + z


def partner_pairs(phase, mask):
    pairs = []
    for x in range(4):
        for c in range(2):
            for y in range(4):
                for z in range(4):
                    other = (y ^ mask, z) if phase != c else (y, z ^ mask)
                    pairs.append((linear(x, c, y, z), linear(x, c, *other)))
    return pairs


def exchange(v, phase, mask):
    return lax.ppermute(v, AXES, partner_pairs(phase, mask))


def core_swap(v):
    return lax.ppermute(v, "c", [(0, 1), (1, 0)])


MASKS = (1, 3, 2)
SMEM = pl.BlockSpec(memory_space=pltpu.SMEM)
VMEM = pl.BlockSpec(memory_space=pltpu.VMEM)


def few(mib):
    return pltpu.CompilerParams(vmem_limit_bytes=mib * 1024 * 1024)


def block(i, n):
    return pl.ds(pl.multiple_of(i * n, 16), n)


def lanes(i):
    return pl.ds(pl.multiple_of(i * 128, 128), 128)


def split_kernel(c_ref, t_ref, out_ref):
    c = c_ref[0]
    for x in range(4):
        out_ref[:, x * 128 : (x + 1) * 128] = t_ref[:, lanes(2 * x + 1 - c)]
        out_ref[:, (x + 4) * 128 : (x + 5) * 128] = t_ref[:, lanes(2 * x + c)]


def split_cores(c, t):
    return pl.pallas_call(
        split_kernel,
        compiler_params=few(2), in_specs=[SMEM, VMEM], out_specs=VMEM, out_shape=jax.ShapeDtypeStruct(t.shape, t.dtype)
    )(c.reshape(1), t)


def merge_kernel(c_ref, *refs):
    c, terms, out_ref = c_ref[0], refs[:-1], refs[-1]
    for x in range(8):
        total = sum(t[:, x * 128 : (x + 1) * 128].astype(F32) for t in terms)
        out_ref[:, lanes(2 * (x % 4) + (c if x >= 4 else 1 - c))] = total.astype(BF16)


def merge_cores(c, *terms):
    return pl.pallas_call(
        merge_kernel,
        compiler_params=few(6),
        in_specs=[SMEM] + [VMEM] * len(terms),
        out_specs=VMEM,
        out_shape=jax.ShapeDtypeStruct(terms[0].shape, BF16),
    )(c.reshape(1), *terms)


def join_kernel(a_ref, b_ref, out_ref):
    out_ref[: a_ref.shape[0], :] = a_ref[...]
    out_ref[a_ref.shape[0] :, :] = b_ref[...]


def join(a, b):
    return pl.pallas_call(
        join_kernel,
        compiler_params=few(6),
        in_specs=[VMEM] * 2,
        out_specs=VMEM,
        out_shape=jax.ShapeDtypeStruct((2 * a.shape[0], a.shape[1]), a.dtype),
    )(a, b)


def add_products_kernel(side, at_ref, part_ref, *refs):
    *pieces, w_ref, out_ref = refs
    m, n = out_ref.shape
    k = pieces[0].shape[0]
    for i in range(0, m, 256):
        at = slice(side * m + i, side * m + i + 256)
        turned = [piece[:, at].T for piece in pieces]
        for j in range(0, n, 256):
            to = slice(j, min(j + 256, n))
            total = part_ref[i : i + 256, to] if part_ref.shape[0] == m else part_ref[at, to]
            for p, piece in enumerate(turned):
                w = w_ref[pl.ds(pl.multiple_of(at_ref[p], 16), k), to]
                total += jnp.dot(piece, w, preferred_element_type=F32)
            out_ref[i : i + 256, to] = total.astype(out_ref.dtype)


def add_products(starts, part, pieces, w, rows, side=0, dtype=F32):
    return pl.pallas_call(
        functools.partial(add_products_kernel, side),
        compiler_params=few(16),
        in_specs=[SMEM] + [VMEM] * (2 + len(pieces)),
        out_specs=VMEM,
        out_shape=jax.ShapeDtypeStruct((rows, part.shape[1]), dtype),
        cost_estimate=pl.CostEstimate(flops=0, bytes_accessed=0, transcendentals=0),
    )(jnp.stack(starts), part, *pieces, w)


def in_halves(i, n, use):
    for half in range(2):

        @pl.when(i // 2 == half)
        def _():
            use(half, block(i - 2 * half, n))


def assemble_kernel(at_ref, *refs):
    n = refs[0].shape[0]
    for p in range(4):

        def put(half, at):
            refs[4 + half][at, :] = refs[p][...]

        in_halves(at_ref[p], n, put)


def assemble(places, *pieces):
    n, m = pieces[0].shape
    return pl.pallas_call(
        assemble_kernel,
        compiler_params=few(6),
        in_specs=[SMEM] + [VMEM] * 4,
        out_specs=[VMEM] * 2,
        out_shape=[jax.ShapeDtypeStruct((2 * n, m), BF16)] * 2,
    )(jnp.stack(places), *pieces)


def part_kernel(at_ref, *refs):
    terms, outs = (refs[:3], refs[3:6]), refs[6:]
    n = outs[0].shape[0]
    for p in range(4):

        def put(half, at):
            outs[p][...] = sum(t[at, :].astype(F32) for t in terms[half]).astype(BF16)

        in_halves(at_ref[p], n, put)


def add_and_part(places, *terms):
    n, m = terms[0].shape
    return pl.pallas_call(
        part_kernel,
        compiler_params=few(12),
        in_specs=[SMEM] + [VMEM] * 6,
        out_specs=[VMEM] * 4,
        out_shape=[jax.ShapeDtypeStruct((n // 2, m), BF16)] * 4,
    )(jnp.stack(places), *terms)


def shards(tokens, w_query, w_keyvalue, w_output, key_cache, value_cache):
    c = lax.axis_index("c")
    column = lax.axis_index("y") * 4 + lax.axis_index("z")
    rows_dev, _, head_size = key_cache.shape
    feat = tokens.shape[1]
    kv_cols = w_keyvalue.shape[1] // 16
    q_cols = w_query.shape[1]

    y, z = lax.axis_index("y"), lax.axis_index("z")
    first, second = jnp.where(c == 0, z, y), jnp.where(c == 0, y, z)
    firsts, seconds = [first ^ m for m in (0, *MASKS)], [second ^ m for m in (0, *MASKS)]

    t = split_cores(c, tokens.T)
    low, high = assemble(firsts, t, *[exchange(t, 0, m) for m in MASKS])
    half = low.shape[0]
    def by_blocks(w):
        w = w.reshape(4, 4, feat, -1)
        return jnp.where(c == 0, w, w.swapaxes(0, 1)).reshape(16 * feat, -1)

    kv_own = lax.dynamic_slice_in_dim(w_keyvalue, column * kv_cols, kv_cols, 1)
    w_all = by_blocks(jnp.concatenate([w_query, jnp.pad(kv_own, ((0, 0), (0, 128 - kv_cols)))], 1))
    w_out = by_blocks(lax.optimization_barrier(w_output.T))

    def product(v, i, skip=0):
        w = lax.dynamic_slice_in_dim(w_all, i * 4 * feat + skip, v.shape[0], 0)
        return lax.dot_general(v, w, (((0,), (0,)), ((), ())), preferred_element_type=F32)

    high1, low3 = exchange(high, 1, 1), exchange(low, 1, 3)
    part = product(low, seconds[0]) + product(high, seconds[0], half)
    low, high, part = lax.optimization_barrier((low, high, part))
    low1, high3 = exchange(low, 1, 1), exchange(high, 1, 3)
    low2, high2 = exchange(low3, 1, 1), exchange(high1, 1, 3)
    part = part + product(high1, seconds[1], half) + product(low3, seconds[2])
    starts = [seconds[1] * 2 * half, seconds[2] * 2 * half + half, seconds[3] * 2 * half, seconds[3] * 2 * half + half]
    part = add_products(starts[:2], part, (low1, high3), w_all, 1024)
    last = low2, high2
    given = core_swap(add_products(starts[2:], part, last, w_all, 512, 0, BF16))
    part = add_products(starts[2:], part, last, w_all, 512, 1)
    part = (part + given.astype(F32)).astype(BF16)
    part = lax.all_to_all(part.reshape(64, rows_dev, -1), ("x", "y", "z"), 0, 0, tiled=True)
    whole = jnp.sum(part.astype(F32).reshape(4, 16, rows_dev, -1), axis=0).astype(BF16)
    queries = whole[:, :, :q_cols].transpose(1, 0, 2).reshape(rows_dev, -1, head_size)
    new_keyvalue = whole[:, :, q_cols : q_cols + kv_cols].transpose(1, 0, 2).reshape(rows_dev, -1)

    new_key = new_keyvalue[:, :head_size]
    new_value = new_keyvalue[:, head_size:]
    score_scale = 1.0 / head_size**0.5
    scores = jnp.einsum("bhe,bte->bht", queries, key_cache, preferred_element_type=F32) * score_scale
    score_new = jnp.einsum("bhe,be->bh", queries, new_key, preferred_element_type=F32) * score_scale
    highest = jnp.maximum(jnp.max(scores, axis=2), score_new)
    raised = jnp.exp(scores - highest[:, :, None])
    raised_new = jnp.exp(score_new - highest)
    denominator = jnp.sum(raised, axis=2) + raised_new
    probs = (raised / denominator[:, :, None]).astype(BF16)
    prob_new = (raised_new / denominator).astype(BF16)
    mixed = jnp.einsum("bht,bte->bhe", probs, value_cache, preferred_element_type=F32)
    mixed = mixed + prob_new.astype(F32)[:, :, None] * new_value.astype(F32)[:, None, :]
    attended = mixed.astype(BF16).reshape(rows_dev, 16, q_cols).transpose(1, 0, 2)

    spread = jnp.broadcast_to(attended[None], (4, 16, rows_dev, q_cols)).reshape(64, rows_dev, q_cols)
    mine = lax.all_to_all(spread, ("x", "y", "z"), 0, 0, tiled=True).reshape(512, q_cols)
    mine, w_out = lax.optimization_barrier((mine, w_out))
    rows = join(core_swap(mine), mine)

    def outward(i, skip):
        w = lax.dynamic_slice_in_dim(w_out, i * 4 * feat + skip, half, 0)
        return lax.dot_general(w, rows, (((1,), (1,)), ((), ())), preferred_element_type=F32)

    def send(v, mask):
        return exchange(v.astype(BF16), 1, mask)

    low2, high2 = send(outward(seconds[3], 0), 1), send(outward(seconds[3], half), 3)
    low1, high3 = send(outward(seconds[1], 0), 1), send(outward(seconds[2], half), 3)
    high1, low3 = send(outward(seconds[1], half) + high2.astype(F32), 1), send(outward(seconds[2], 0) + low2.astype(F32), 3)
    low, high = outward(seconds[0], 0).astype(BF16), outward(seconds[0], half).astype(BF16)
    keep, *away = add_and_part(firsts, low, low1, low3, high, high1, high3)
    out = merge_cores(c, keep, *[exchange(v, 0, m) for v, m in zip(away, MASKS)])
    return out.T, new_keyvalue


def solution(mesh):
    fine = Mesh(mesh.devices.reshape(4, 2, 4, 4), AXES)
    gx, gy = ("x", "c"), ("y", "z")
    every = (*gx, *gy)
    return jax.shard_map(
        shards,
        mesh=fine,
        in_specs=(P(None, every), P(gx, gy), P(gx, None), P(gy, gx), P(every, None, None), P(every, None, None)),
        out_specs=(P(None, every), P(every, None)),
        check_vma=False,
    )
```

```python
import functools

import jax
import jax.numpy as jnp
from jax import lax
from jax.experimental import pallas as pl
from jax.experimental.pallas import tpu as pltpu
from jax.sharding import Mesh
from jax.sharding import PartitionSpec as P

AXES = ("x", "c", "y", "z")
F32 = jnp.float32
BF16 = jnp.bfloat16


def linear(x, c, y, z):
    return ((x * 2 + c) * 4 + y) * 4 + z


def partner_pairs(phase, mask):
    pairs = []
    for x in range(4):
        for c in range(2):
            for y in range(4):
                for z in range(4):
                    other = (y ^ mask, z) if phase != c else (y, z ^ mask)
                    pairs.append((linear(x, c, y, z), linear(x, c, *other)))
    return pairs


def exchange(v, phase, mask):
    return lax.ppermute(v, AXES, partner_pairs(phase, mask))


def core_swap(v):
    return lax.ppermute(v, "c", [(0, 1), (1, 0)])


MASKS = (2, 1, 3)
SMEM = pl.BlockSpec(memory_space=pltpu.SMEM)
VMEM = pl.BlockSpec(memory_space=pltpu.VMEM)


def few(mib):
    return pltpu.CompilerParams(vmem_limit_bytes=mib * 1024 * 1024)


def block(i, n):
    return pl.ds(pl.multiple_of(i * n, 16), n)


def lanes(i):
    return pl.ds(pl.multiple_of(i * 128, 128), 128)


def merge_kernel(c_ref, *refs):
    c, terms, out_ref = c_ref[0], refs[:-1], refs[-1]
    for x in range(8):
        total = sum(t[:, x * 128 : (x + 1) * 128].astype(F32) for t in terms)
        out_ref[:, lanes(2 * (x % 4) + (c if x >= 4 else 1 - c))] = total.astype(BF16)


def merge_cores(c, *terms):
    return pl.pallas_call(
        merge_kernel,
        compiler_params=few(6),
        in_specs=[SMEM] + [VMEM] * len(terms),
        out_specs=VMEM,
        out_shape=jax.ShapeDtypeStruct(terms[0].shape, BF16),
    )(c.reshape(1), *terms)


def add_products_kernel(at_ref, part_ref, *refs):
    *pieces, w_ref, out_ref = refs
    m, n = out_ref.shape
    k = pieces[0].shape[0]
    step = part_ref.shape[0] // m
    for i in range(0, m // 128, 2):
        blocks = [lanes(step * (i + d) + at_ref[0]) for d in range(2)]
        turned = [jnp.concatenate([piece[:, b].T for b in blocks], 0) for piece in pieces]
        for j in range(0, n, 256):
            to = slice(j, min(j + 256, n))
            total = jnp.concatenate([part_ref[b, to] for b in blocks], 0)
            for p, piece in enumerate(turned):
                w = w_ref[pl.ds(pl.multiple_of(at_ref[1 + p], 16), k), to]
                total += jnp.dot(piece, w, preferred_element_type=F32)
            out_ref[i * 128 : (i + 2) * 128, to] = total.astype(out_ref.dtype)


def add_products(side, starts, part, pieces, w, rows, dtype=F32):
    return pl.pallas_call(
        add_products_kernel,
        compiler_params=few(16),
        in_specs=[SMEM] + [VMEM] * (2 + len(pieces)),
        out_specs=VMEM,
        out_shape=jax.ShapeDtypeStruct((rows, part.shape[1]), dtype),
        cost_estimate=pl.CostEstimate(flops=0, bytes_accessed=0, transcendentals=0),
    )(jnp.stack([side, *starts]), part, *pieces, w)


def join_kernel(a_ref, b_ref, out_ref):
    out_ref[: a_ref.shape[0], :] = a_ref[...]
    out_ref[a_ref.shape[0] :, :] = b_ref[...]


def join(a, b):
    return pl.pallas_call(
        join_kernel,
        compiler_params=few(6),
        in_specs=[VMEM] * 2,
        out_specs=VMEM,
        out_shape=jax.ShapeDtypeStruct((2 * a.shape[0], a.shape[1]), a.dtype),
    )(a, b)


def in_halves(i, n, use):
    for half in range(2):

        @pl.when(i // 2 == half)
        def _():
            use(half, block(i - 2 * half, n))


def assemble_kernel(at_ref, *refs):
    n = refs[0].shape[0]
    for p in range(4):

        def put(half, at):
            refs[4 + half][at, :] = refs[p][...]

        in_halves(at_ref[p], n, put)


def assemble(places, *pieces):
    n, m = pieces[0].shape
    return pl.pallas_call(
        assemble_kernel,
        compiler_params=few(6),
        in_specs=[SMEM] + [VMEM] * 4,
        out_specs=[VMEM] * 2,
        out_shape=[jax.ShapeDtypeStruct((2 * n, m), BF16)] * 2,
    )(jnp.stack(places), *pieces)


def part_kernel(at_ref, *refs):
    terms, outs = (refs[:3], refs[3:6]), refs[6:]
    n = outs[0].shape[0]
    for p in range(4):

        def put(half, at):
            outs[p][...] = sum(t[at, :].astype(F32) for t in terms[half]).astype(BF16)

        in_halves(at_ref[p], n, put)


def add_and_part(places, *terms):
    n, m = terms[0].shape
    return pl.pallas_call(
        part_kernel,
        compiler_params=few(12),
        in_specs=[SMEM] + [VMEM] * 6,
        out_specs=[VMEM] * 4,
        out_shape=[jax.ShapeDtypeStruct((n // 2, m), BF16)] * 4,
    )(jnp.stack(places), *terms)


def shards(tokens, w_query, w_keyvalue, w_output, key_cache, value_cache):
    c = lax.axis_index("c")
    column = lax.axis_index("y") * 4 + lax.axis_index("z")
    rows_dev, _, head_size = key_cache.shape
    feat = tokens.shape[1]
    kv_cols = w_keyvalue.shape[1] // 16
    q_cols = w_query.shape[1]

    y, z = lax.axis_index("y"), lax.axis_index("z")
    first, second = jnp.where(c == 0, z, y), jnp.where(c == 0, y, z)
    firsts, seconds = [first ^ m for m in (0, *MASKS)], [second ^ m for m in (0, 1, 3, 2)]

    t = tokens.T
    low, high = assemble(firsts, t, *[exchange(t, 0, m) for m in MASKS])
    half = low.shape[0]
    def by_blocks(w):
        w = w.reshape(4, 4, feat, -1)
        return jnp.where(c == 0, w, w.swapaxes(0, 1)).reshape(16 * feat, -1)

    kv_own = lax.dynamic_slice_in_dim(w_keyvalue, column * kv_cols, kv_cols, 1)
    w_all = by_blocks(jnp.concatenate([w_query, jnp.pad(kv_own, ((0, 0), (0, 128 - kv_cols)))], 1))
    w_out = by_blocks(lax.optimization_barrier(w_output.T))

    def product(v, i, skip=0):
        w = lax.dynamic_slice_in_dim(w_all, i * 4 * feat + skip, v.shape[0], 0)
        return lax.dot_general(v, w, (((0,), (0,)), ((), ())), preferred_element_type=F32)

    high1, low3 = exchange(high, 1, 1), exchange(low, 1, 3)
    part = product(low, seconds[0]) + product(high, seconds[0], half)
    low, high, part = lax.optimization_barrier((low, high, part))
    low1, high3 = exchange(low, 1, 1), exchange(high, 1, 3)
    low2, high2 = exchange(low3, 1, 1), exchange(high1, 1, 3)
    part = part + product(high1, seconds[1], half) + product(low3, seconds[2])
    starts = [seconds[1] * 2 * half, seconds[2] * 2 * half + half, seconds[3] * 2 * half, seconds[3] * 2 * half + half]
    none = jnp.zeros_like(c)
    part = add_products(none, starts[:2], part, (low1, high3), w_all, 1024)
    last = low2, high2
    given = core_swap(add_products(1 - c, starts[2:], part, last, w_all, 512, BF16))
    part = add_products(c, starts[2:], part, last, w_all, 512)
    part = (part + given.astype(F32)).astype(BF16)
    part = lax.all_to_all(part.reshape(64, rows_dev, -1), ("x", "y", "z"), 0, 0, tiled=True)
    whole = jnp.sum(part.astype(F32).reshape(4, 16, rows_dev, -1), axis=0).astype(BF16)
    queries = whole[:, :, :q_cols].transpose(1, 0, 2).reshape(rows_dev, -1, head_size)
    new_keyvalue = whole[:, :, q_cols : q_cols + kv_cols].transpose(1, 0, 2).reshape(rows_dev, -1)

    new_key = new_keyvalue[:, :head_size]
    new_value = new_keyvalue[:, head_size:]
    score_scale = 1.0 / head_size**0.5
    scores = jnp.einsum("bhe,bte->bht", queries, key_cache, preferred_element_type=F32) * score_scale
    score_new = jnp.einsum("bhe,be->bh", queries, new_key, preferred_element_type=F32) * score_scale
    highest = jnp.maximum(jnp.max(scores, axis=2), score_new)
    raised = jnp.exp(scores - highest[:, :, None])
    raised_new = jnp.exp(score_new - highest)
    denominator = jnp.sum(raised, axis=2) + raised_new
    probs = (raised / denominator[:, :, None]).astype(BF16)
    prob_new = (raised_new / denominator).astype(BF16)
    mixed = jnp.einsum("bht,bte->bhe", probs, value_cache, preferred_element_type=F32)
    mixed = mixed + prob_new.astype(F32)[:, :, None] * new_value.astype(F32)[:, None, :]
    attended = mixed.astype(BF16).reshape(rows_dev, 16, q_cols).transpose(1, 0, 2)

    spread = jnp.broadcast_to(attended[None], (4, 16, rows_dev, q_cols)).reshape(64, rows_dev, q_cols)
    mine = lax.all_to_all(spread, ("x", "y", "z"), 0, 0, tiled=True).reshape(512, q_cols)
    mine, w_out = lax.optimization_barrier((mine, w_out))
    theirs = core_swap(mine)
    rows = join(theirs, mine)

    def outward(i, skip, rows=rows):
        w = lax.dynamic_slice_in_dim(w_out, i * 4 * feat + skip, half, 0)
        return lax.dot_general(w, rows, (((1,), (1,)), ((), ())), preferred_element_type=F32)

    def send(v, mask):
        return exchange(v.astype(BF16), 1, mask)

    low2, high2 = send(outward(seconds[3], 0), 1), send(outward(seconds[3], half), 3)
    low1, high3 = send(outward(seconds[1], 0), 1), send(outward(seconds[2], half), 3)
    high1, low3 = send(outward(seconds[1], half) + high2.astype(F32), 1), send(outward(seconds[2], 0) + low2.astype(F32), 3)
    low, high = outward(seconds[0], 0).astype(BF16), outward(seconds[0], half).astype(BF16)
    keep, *away = add_and_part(firsts, low, low1, low3, high, high1, high3)
    out = merge_cores(c, keep, *[exchange(v, 0, m) for v, m in zip(away, MASKS)])
    return out.T, new_keyvalue


def solution(mesh):
    fine = Mesh(mesh.devices.reshape(4, 2, 4, 4), AXES)
    gx, gy = ("x", "c"), ("y", "z")
    every = (*gx, *gy)
    return jax.shard_map(
        shards,
        mesh=fine,
        in_specs=(P(None, every), P(gx, gy), P(gx, None), P(gy, gx), P(every, None, None), P(every, None, None)),
        out_specs=(P(None, every), P(every, None)),
        check_vma=False,
    )
```

```python
import functools

import jax
import jax.numpy as jnp
from jax import lax
from jax.experimental import pallas as pl
from jax.experimental.pallas import tpu as pltpu
from jax.sharding import Mesh
from jax.sharding import PartitionSpec as P

AXES = ("x", "c", "y", "z")
F32 = jnp.float32
BF16 = jnp.bfloat16


def linear(x, c, y, z):
    return ((x * 2 + c) * 4 + y) * 4 + z


def partner_pairs(phase, mask):
    pairs = []
    for x in range(4):
        for c in range(2):
            for y in range(4):
                for z in range(4):
                    other = (y ^ mask, z) if phase != c else (y, z ^ mask)
                    pairs.append((linear(x, c, y, z), linear(x, c, *other)))
    return pairs


def exchange(v, phase, mask):
    return lax.ppermute(v, AXES, partner_pairs(phase, mask))


def core_swap(v):
    return lax.ppermute(v, "c", [(0, 1), (1, 0)])


MASKS = (2, 1, 3)
SMEM = pl.BlockSpec(memory_space=pltpu.SMEM)
VMEM = pl.BlockSpec(memory_space=pltpu.VMEM)


def few(mib):
    return pltpu.CompilerParams(vmem_limit_bytes=mib * 1024 * 1024)


def block(i, n):
    return pl.ds(pl.multiple_of(i * n, 16), n)


def lanes(i):
    return pl.ds(pl.multiple_of(i * 128, 128), 128)


def merge_kernel(c_ref, *refs):
    c, terms, out_ref = c_ref[0], refs[:-1], refs[-1]
    for x in range(8):
        total = sum(t[:, x * 128 : (x + 1) * 128].astype(F32) for t in terms)
        out_ref[:, lanes(2 * (x % 4) + (c if x >= 4 else 1 - c))] = total.astype(BF16)


def merge_cores(c, *terms):
    return pl.pallas_call(
        merge_kernel,
        compiler_params=few(6),
        in_specs=[SMEM] + [VMEM] * len(terms),
        out_specs=VMEM,
        out_shape=jax.ShapeDtypeStruct(terms[0].shape, BF16),
    )(c.reshape(1), *terms)


def add_products_kernel(at_ref, part_ref, *refs):
    *pieces, w_ref, out_ref = refs
    m, n = out_ref.shape
    k = pieces[0].shape[0]
    step = part_ref.shape[0] // m
    for i in range(0, m // 128, 2):
        blocks = [lanes(step * (i + d) + at_ref[0]) for d in range(2)]
        turned = [jnp.concatenate([piece[:, b].T for b in blocks], 0) for piece in pieces]
        for j in range(0, n, 256):
            to = slice(j, min(j + 256, n))
            total = jnp.concatenate([part_ref[b, to] for b in blocks], 0)
            for p, piece in enumerate(turned):
                w = w_ref[pl.ds(pl.multiple_of(at_ref[1 + p], 16), k), to]
                total += jnp.dot(piece, w, preferred_element_type=F32)
            out_ref[i * 128 : (i + 2) * 128, to] = total.astype(out_ref.dtype)


def add_products(side, starts, part, pieces, w, rows, dtype=F32):
    return pl.pallas_call(
        add_products_kernel,
        compiler_params=few(16),
        in_specs=[SMEM] + [VMEM] * (2 + len(pieces)),
        out_specs=VMEM,
        out_shape=jax.ShapeDtypeStruct((rows, part.shape[1]), dtype),
        cost_estimate=pl.CostEstimate(flops=0, bytes_accessed=0, transcendentals=0),
    )(jnp.stack([side, *starts]), part, *pieces, w)


def join_kernel(a_ref, b_ref, out_ref):
    out_ref[: a_ref.shape[0], :] = a_ref[...]
    out_ref[a_ref.shape[0] :, :] = b_ref[...]


def join(a, b):
    return pl.pallas_call(
        join_kernel,
        compiler_params=few(6),
        in_specs=[VMEM] * 2,
        out_specs=VMEM,
        out_shape=jax.ShapeDtypeStruct((2 * a.shape[0], a.shape[1]), a.dtype),
    )(a, b)


def in_halves(i, n, use):
    for half in range(2):

        @pl.when(i // 2 == half)
        def _():
            use(half, block(i - 2 * half, n))


def assemble_kernel(at_ref, *refs):
    n = refs[0].shape[0]
    for p in range(4):

        def put(half, at):
            refs[4 + half][at, :] = refs[p][...]

        in_halves(at_ref[p], n, put)


def assemble(places, *pieces):
    n, m = pieces[0].shape
    return pl.pallas_call(
        assemble_kernel,
        compiler_params=few(6),
        in_specs=[SMEM] + [VMEM] * 4,
        out_specs=[VMEM] * 2,
        out_shape=[jax.ShapeDtypeStruct((2 * n, m), BF16)] * 2,
    )(jnp.stack(places), *pieces)


def part_kernel(at_ref, *refs):
    terms, outs = (refs[:3], refs[3:6]), refs[6:]
    n = outs[0].shape[0]
    for p in range(4):

        def put(half, at):
            outs[p][...] = sum(t[at, :].astype(F32) for t in terms[half]).astype(BF16)

        in_halves(at_ref[p], n, put)


def add_and_part(places, *terms):
    n, m = terms[0].shape
    return pl.pallas_call(
        part_kernel,
        compiler_params=few(12),
        in_specs=[SMEM] + [VMEM] * 6,
        out_specs=[VMEM] * 4,
        out_shape=[jax.ShapeDtypeStruct((n // 2, m), BF16)] * 4,
    )(jnp.stack(places), *terms)


def shards(tokens, w_query, w_keyvalue, w_output, key_cache, value_cache):
    c = lax.axis_index("c")
    column = lax.axis_index("y") * 4 + lax.axis_index("z")
    rows_dev, _, head_size = key_cache.shape
    feat = tokens.shape[1]
    kv_cols = w_keyvalue.shape[1] // 16
    q_cols = w_query.shape[1]

    y, z = lax.axis_index("y"), lax.axis_index("z")
    first, second = jnp.where(c == 0, z, y), jnp.where(c == 0, y, z)
    firsts, seconds = [first ^ m for m in (0, *MASKS)], [second ^ m for m in (0, 1, 3, 2)]

    t = tokens.T
    low, high = assemble(firsts, t, *[exchange(t, 0, m) for m in MASKS])
    half = low.shape[0]
    def by_blocks(w):
        w = w.reshape(4, 4, feat, -1)
        return jnp.where(c == 0, w, w.swapaxes(0, 1)).reshape(16 * feat, -1)

    kv_own = lax.dynamic_slice_in_dim(w_keyvalue, column * kv_cols, kv_cols, 1)
    w_all = by_blocks(jnp.concatenate([w_query, jnp.pad(kv_own, ((0, 0), (0, 128 - kv_cols)))], 1))
    w_out = by_blocks(lax.optimization_barrier(w_output.T))

    def product(v, i, skip=0):
        w = lax.dynamic_slice_in_dim(w_all, i * 4 * feat + skip, v.shape[0], 0)
        return lax.dot_general(v, w, (((0,), (0,)), ((), ())), preferred_element_type=F32)

    high1, low3 = exchange(high, 1, 1), exchange(low, 1, 3)
    part = product(low, seconds[0]) + product(high, seconds[0], half)
    low, high, part = lax.optimization_barrier((low, high, part))
    low1, high3 = exchange(low, 1, 1), exchange(high, 1, 3)
    low2, high2 = exchange(low3, 1, 1), exchange(high1, 1, 3)
    part = part + product(high1, seconds[1], half) + product(low3, seconds[2])
    starts = [seconds[1] * 2 * half, seconds[2] * 2 * half + half, seconds[3] * 2 * half, seconds[3] * 2 * half + half]
    none = jnp.zeros_like(c)
    part = add_products(none, starts[:2], part, (low1, high3), w_all, 1024)
    last = low2, high2
    given = core_swap(add_products(1 - c, starts[2:], part, last, w_all, 512, BF16))
    part = add_products(c, starts[2:], part, last, w_all, 512)
    part = (part + given.astype(F32)).astype(BF16)
    part = lax.all_to_all(part.reshape(64, rows_dev, -1), ("x", "y", "z"), 0, 0, tiled=True)
    whole = jnp.sum(part.astype(F32).reshape(4, 16, rows_dev, -1), axis=0).astype(BF16)
    queries = whole[:, :, :q_cols].transpose(1, 0, 2).reshape(rows_dev, -1, head_size)
    new_keyvalue = whole[:, :, q_cols : q_cols + kv_cols].transpose(1, 0, 2).reshape(rows_dev, -1)

    new_key = new_keyvalue[:, :head_size]
    new_value = new_keyvalue[:, head_size:]
    score_scale = 1.0 / head_size**0.5
    scores = jnp.einsum("bhe,bte->bht", queries, key_cache, preferred_element_type=F32) * score_scale
    score_new = jnp.einsum("bhe,be->bh", queries, new_key, preferred_element_type=F32) * score_scale
    highest = jnp.maximum(jnp.max(scores, axis=2), score_new)
    raised = jnp.exp(scores - highest[:, :, None])
    raised_new = jnp.exp(score_new - highest)
    denominator = jnp.sum(raised, axis=2) + raised_new
    probs = (raised / denominator[:, :, None]).astype(BF16)
    prob_new = (raised_new / denominator).astype(BF16)
    mixed = jnp.einsum("bht,bte->bhe", probs, value_cache, preferred_element_type=F32)
    mixed = mixed + prob_new.astype(F32)[:, :, None] * new_value.astype(F32)[:, None, :]
    attended = mixed.astype(BF16).reshape(rows_dev, 16, q_cols).transpose(1, 0, 2)

    spread = jnp.broadcast_to(attended[None], (4, 16, rows_dev, q_cols)).reshape(64, rows_dev, q_cols)
    mine = lax.all_to_all(spread, ("x", "y", "z"), 0, 0, tiled=True).reshape(512, q_cols)
    far = [lax.dynamic_slice_in_dim(w_out, seconds[3] * 4 * feat + skip, half, 0) for skip in (0, half)]
    mine, w_out, far = lax.optimization_barrier((mine, w_out, far))
    theirs = core_swap(mine)
    rows = join(theirs, mine)

    def times(w, rows=rows):
        return lax.dot_general(w, rows, (((1,), (1,)), ((), ())), preferred_element_type=F32)

    def outward(i, skip):
        return times(lax.dynamic_slice_in_dim(w_out, i * 4 * feat + skip, half, 0))

    def send(v, mask):
        return exchange(v.astype(BF16), 1, mask)

    low2, high2 = send(times(far[0]), 1), send(times(far[1]), 3)
    low1, high3 = send(outward(seconds[1], 0), 1), send(outward(seconds[2], half), 3)
    high1, low3 = send(outward(seconds[1], half) + high2.astype(F32), 1), send(outward(seconds[2], 0) + low2.astype(F32), 3)
    low, high = outward(seconds[0], 0).astype(BF16), outward(seconds[0], half).astype(BF16)
    keep, *away = add_and_part(firsts, low, low1, low3, high, high1, high3)
    out = merge_cores(c, keep, *[exchange(v, 0, m) for v, m in zip(away, MASKS)])
    return out.T, new_keyvalue


def solution(mesh):
    fine = Mesh(mesh.devices.reshape(4, 2, 4, 4), AXES)
    gx, gy = ("x", "c"), ("y", "z")
    every = (*gx, *gy)
    return jax.shard_map(
        shards,
        mesh=fine,
        in_specs=(P(None, every), P(gx, gy), P(gx, None), P(gy, gx), P(every, None, None), P(every, None, None)),
        out_specs=(P(None, every), P(every, None)),
        check_vma=False,
    )
```

```python
import functools

import jax
import jax.numpy as jnp
from jax import lax
from jax.experimental import pallas as pl
from jax.experimental.pallas import tpu as pltpu
from jax.sharding import Mesh
from jax.sharding import PartitionSpec as P

AXES = ("x", "c", "y", "z")
F32 = jnp.float32
BF16 = jnp.bfloat16


def linear(x, c, y, z):
    return ((x * 2 + c) * 4 + y) * 4 + z


def partner_pairs(phase, mask):
    pairs = []
    for x in range(4):
        for c in range(2):
            for y in range(4):
                for z in range(4):
                    other = (y ^ mask, z) if phase != c else (y, z ^ mask)
                    pairs.append((linear(x, c, y, z), linear(x, c, *other)))
    return pairs


def exchange(v, phase, mask):
    return lax.ppermute(v, AXES, partner_pairs(phase, mask))


def core_swap(v):
    return lax.ppermute(v, "c", [(0, 1), (1, 0)])


MASKS = (2, 1, 3)
SMEM = pl.BlockSpec(memory_space=pltpu.SMEM)
VMEM = pl.BlockSpec(memory_space=pltpu.VMEM)


def few(mib):
    return pltpu.CompilerParams(vmem_limit_bytes=mib * 1024 * 1024)


def block(i, n):
    return pl.ds(pl.multiple_of(i * n, 16), n)


def lanes(i):
    return pl.ds(pl.multiple_of(i * 128, 128), 128)


def merge_kernel(c_ref, *refs):
    c, terms, out_ref = c_ref[0], refs[:-1], refs[-1]
    for x in range(8):
        total = sum(t[:, x * 128 : (x + 1) * 128].astype(F32) for t in terms)
        out_ref[:, lanes(2 * (x % 4) + (c if x >= 4 else 1 - c))] = total.astype(BF16)


def merge_cores(c, *terms):
    return pl.pallas_call(
        merge_kernel,
        compiler_params=few(6),
        in_specs=[SMEM] + [VMEM] * len(terms),
        out_specs=VMEM,
        out_shape=jax.ShapeDtypeStruct(terms[0].shape, BF16),
    )(c.reshape(1), *terms)


def add_products_kernel(at_ref, part_ref, *refs):
    *pieces, w_ref, out_ref = refs
    m, n = out_ref.shape
    k = pieces[0].shape[0]
    step = part_ref.shape[0] // m
    for i in range(0, m // 128, 2):
        blocks = [lanes(step * (i + d) + at_ref[0]) for d in range(2)]
        turned = [jnp.concatenate([piece[:, b].T for b in blocks], 0) for piece in pieces]
        for j in range(0, n, 256):
            to = slice(j, min(j + 256, n))
            total = jnp.concatenate([part_ref[b, to] for b in blocks], 0)
            for p, piece in enumerate(turned):
                w = w_ref[pl.ds(pl.multiple_of(at_ref[1 + p], 16), k), to]
                total += jnp.dot(piece, w, preferred_element_type=F32)
            out_ref[i * 128 : (i + 2) * 128, to] = total.astype(out_ref.dtype)


def add_products(side, starts, part, pieces, w, rows, dtype=F32):
    return pl.pallas_call(
        add_products_kernel,
        compiler_params=few(16),
        in_specs=[SMEM] + [VMEM] * (2 + len(pieces)),
        out_specs=VMEM,
        out_shape=jax.ShapeDtypeStruct((rows, part.shape[1]), dtype),
        cost_estimate=pl.CostEstimate(flops=0, bytes_accessed=0, transcendentals=0),
    )(jnp.stack([side, *starts]), part, *pieces, w)


def join_kernel(a_ref, b_ref, out_ref):
    out_ref[: a_ref.shape[0], :] = a_ref[...]
    out_ref[a_ref.shape[0] :, :] = b_ref[...]


def join(a, b):
    return pl.pallas_call(
        join_kernel,
        compiler_params=few(6),
        in_specs=[VMEM] * 2,
        out_specs=VMEM,
        out_shape=jax.ShapeDtypeStruct((2 * a.shape[0], a.shape[1]), a.dtype),
    )(a, b)


def in_halves(i, n, use):
    for half in range(2):

        @pl.when(i // 2 == half)
        def _():
            use(half, block(i - 2 * half, n))


def assemble_kernel(at_ref, *refs):
    n = refs[0].shape[0]
    for p in range(4):

        def put(half, at):
            refs[4 + half][at, :] = refs[p][...]

        in_halves(at_ref[p], n, put)


def assemble(places, *pieces):
    n, m = pieces[0].shape
    return pl.pallas_call(
        assemble_kernel,
        compiler_params=few(6),
        in_specs=[SMEM] + [VMEM] * 4,
        out_specs=[VMEM] * 2,
        out_shape=[jax.ShapeDtypeStruct((2 * n, m), BF16)] * 2,
    )(jnp.stack(places), *pieces)


def part_kernel(at_ref, *refs):
    terms, outs = (refs[:3], refs[3:6]), refs[6:]
    n = outs[0].shape[0]
    for p in range(4):

        def put(half, at):
            outs[p][...] = sum(t[at, :].astype(F32) for t in terms[half]).astype(BF16)

        in_halves(at_ref[p], n, put)


def add_and_part(places, *terms):
    n, m = terms[0].shape
    return pl.pallas_call(
        part_kernel,
        compiler_params=few(12),
        in_specs=[SMEM] + [VMEM] * 6,
        out_specs=[VMEM] * 4,
        out_shape=[jax.ShapeDtypeStruct((n // 2, m), BF16)] * 4,
    )(jnp.stack(places), *terms)


def shards(tokens, w_query, w_keyvalue, w_output, key_cache, value_cache):
    c = lax.axis_index("c")
    column = lax.axis_index("y") * 4 + lax.axis_index("z")
    rows_dev, _, head_size = key_cache.shape
    feat = tokens.shape[1]
    kv_cols = w_keyvalue.shape[1] // 16
    q_cols = w_query.shape[1]

    y, z = lax.axis_index("y"), lax.axis_index("z")
    first, second = jnp.where(c == 0, z, y), jnp.where(c == 0, y, z)
    firsts, seconds = [first ^ m for m in (0, *MASKS)], [second ^ m for m in (0, 1, 3, 2)]

    t = tokens.T
    low, high = assemble(firsts, t, *[exchange(t, 0, m) for m in MASKS])
    half = low.shape[0]
    def by_blocks(w):
        w = w.reshape(4, 4, feat, -1)
        return jnp.where(c == 0, w, w.swapaxes(0, 1)).reshape(16 * feat, -1)

    kv_own = lax.dynamic_slice_in_dim(w_keyvalue, column * kv_cols, kv_cols, 1)
    w_all = by_blocks(jnp.concatenate([w_query, jnp.pad(kv_own, ((0, 0), (0, 128 - kv_cols)))], 1))
    w_out = by_blocks(lax.optimization_barrier(w_output.T))

    def product(v, i, skip=0):
        w = lax.dynamic_slice_in_dim(w_all, i * 4 * feat + skip, v.shape[0], 0)
        return lax.dot_general(v, w, (((0,), (0,)), ((), ())), preferred_element_type=F32)

    high1, low3 = exchange(high, 1, 1), exchange(low, 1, 3)
    part = product(low, seconds[0]) + product(high, seconds[0], half)
    low, high, part = lax.optimization_barrier((low, high, part))
    low1, high3 = exchange(low, 1, 1), exchange(high, 1, 3)
    low2, high2 = exchange(low3, 1, 1), exchange(high1, 1, 3)
    part = part + product(high1, seconds[1], half) + product(low3, seconds[2])
    starts = [seconds[1] * 2 * half, seconds[2] * 2 * half + half, seconds[3] * 2 * half, seconds[3] * 2 * half + half]
    none = jnp.zeros_like(c)
    part = add_products(none, starts[:2], part, (low1, high3), w_all, 1024)
    last = low2, high2
    given = core_swap(add_products(1 - c, starts[2:], part, last, w_all, 512, BF16))
    part = add_products(c, starts[2:], part, last, w_all, 512)
    part = (part + given.astype(F32)).astype(BF16)
    part = lax.all_to_all(part.reshape(64, rows_dev, -1), ("x", "y", "z"), 0, 0, tiled=True)
    whole = jnp.sum(part.astype(F32).reshape(4, 16, rows_dev, -1), axis=0).astype(BF16)
    queries = whole[:, :, :q_cols].transpose(1, 0, 2).reshape(rows_dev, -1, head_size)
    new_keyvalue = whole[:, :, q_cols : q_cols + kv_cols].transpose(1, 0, 2).reshape(rows_dev, -1)

    new_key = new_keyvalue[:, :head_size]
    new_value = new_keyvalue[:, head_size:]
    score_scale = 1.0 / head_size**0.5
    scores = jnp.einsum("bhe,bte->bht", queries, key_cache, preferred_element_type=F32) * score_scale
    score_new = jnp.einsum("bhe,be->bh", queries, new_key, preferred_element_type=F32) * score_scale
    highest = jnp.maximum(jnp.max(scores, axis=2), score_new)
    raised = jnp.exp(scores - highest[:, :, None])
    raised_new = jnp.exp(score_new - highest)
    denominator = jnp.sum(raised, axis=2) + raised_new
    probs = (raised / denominator[:, :, None]).astype(BF16)
    prob_new = (raised_new / denominator).astype(BF16)
    mixed = jnp.einsum("bht,bte->bhe", probs, value_cache, preferred_element_type=F32)
    mixed = mixed + prob_new.astype(F32)[:, :, None] * new_value.astype(F32)[:, None, :]
    attended = mixed.astype(BF16).reshape(rows_dev, 16, q_cols).transpose(1, 0, 2)

    spread = jnp.broadcast_to(attended[None], (4, 16, rows_dev, q_cols)).reshape(64, rows_dev, q_cols)
    mine = lax.all_to_all(spread, ("x", "y", "z"), 0, 0, tiled=True).reshape(512, q_cols)
    far = [lax.dynamic_slice_in_dim(w_out, seconds[3] * 4 * feat + skip, half, 0) for skip in (0, half)]
    mine, w_out, far = lax.optimization_barrier((mine, w_out, far))
    theirs = core_swap(mine)
    rows = join(theirs, mine)

    def times(w, rows):
        return lax.dot_general(w, rows, (((1,), (1,)), ((), ())), preferred_element_type=F32)

    def outward(i, skip, rows):
        return times(lax.dynamic_slice_in_dim(w_out, i * 4 * feat + skip, half, 0), rows)

    def send(v, mask):
        return exchange(v.astype(BF16), 1, mask)

    def added(v, theirs, mine):
        return v + jnp.concatenate([theirs, mine], 1).astype(F32)

    low_mine, high_mine = send(times(far[0], mine), 1), send(times(far[1], mine), 3)
    low_theirs, high_theirs = times(far[0], theirs).astype(BF16), times(far[1], theirs).astype(BF16)
    low_theirs, high_theirs, rows = lax.optimization_barrier((low_theirs, high_theirs, rows))
    low_theirs, high_theirs = exchange(low_theirs, 1, 1), exchange(high_theirs, 1, 3)
    low1, high3 = send(outward(seconds[1], 0, rows), 1), send(outward(seconds[2], half, rows), 3)
    high1 = send(added(outward(seconds[1], half, rows), high_theirs, high_mine), 1)
    low3 = send(added(outward(seconds[2], 0, rows), low_theirs, low_mine), 3)
    low, high = outward(seconds[0], 0, rows).astype(BF16), outward(seconds[0], half, rows).astype(BF16)
    keep, *away = add_and_part(firsts, low, low1, low3, high, high1, high3)
    out = merge_cores(c, keep, *[exchange(v, 0, m) for v, m in zip(away, MASKS)])
    return out.T, new_keyvalue


def solution(mesh):
    fine = Mesh(mesh.devices.reshape(4, 2, 4, 4), AXES)
    gx, gy = ("x", "c"), ("y", "z")
    every = (*gx, *gy)
    return jax.shard_map(
        shards,
        mesh=fine,
        in_specs=(P(None, every), P(gx, gy), P(gx, None), P(gy, gx), P(every, None, None), P(every, None, None)),
        out_specs=(P(None, every), P(every, None)),
        check_vma=False,
    )
```
